32 devices in a mesh: freq: 8 (over z, x), space: 4 (over y, core).
Axes of the slice: x: 2, y: 2, z: 4, core: 2. Of those that a mesh axis runs over, the one named last changes fastest.
Arguments:
- record: float32 [512, 3, 16384], P('freq', None, 'space'), may hold values from -6 to 6
- area_weight: float32 [16384], P('space'), may hold values from 0.2 to 5
- freq_bins: int32 [8], replicated, may hold values from 0 to 64, as said below
Outputs:
- modes: bfloat16 [8, 8, 2, 3, 16384], P('freq', None, None, None, 'space')
- factor: float32 [8, 2, 8, 8], P('freq')
The draws below stay inside these ranges and needn't reach their ends.
Inputs may be any that keep to these rules, and one draw needn't show every extreme that they name: `freq_bins`: the bins are distinct; bin 0 and bin 128 / 2 are always among them.
All inputs are finite; a program needn't handle non-finite values.
Results may differ from the reference program's by a relative error of at most 0.001.
Values sent between devices are 32-bit elements; how exact they have to be, the bound alone decides.
A program may use at most 128 MiB of HBM per device.

```python
import math
import jax
import jax.numpy as jnp
from jax import lax

PTS = 16384
SAMPLES = 128
HOP = 64
BLOCKS = 8
TIME = 512
FBINS = 8


def draw_freq_bins(key, part):
    key = jax.random.fold_in(key, 7)
    half_len = SAMPLES // 2
    inner = jax.random.permutation(key, half_len - 1).astype(jnp.int32) + 1
    chosen = jnp.concatenate([jnp.array([0, half_len], jnp.int32), inner[:FBINS - 2]])
    order = jax.random.permutation(jax.random.fold_in(key, 1), FBINS)
    return chosen[order]


def shard_levels(rng, dims, cuts, low, largest):
    level, own = 1.0, jax.random.fold_in(rng, 6)
    for dim, parts in cuts:
        steps = jnp.exp(jax.random.uniform(jax.random.fold_in(own, dim), (parts,), jnp.float32, low / len(cuts), largest / len(cuts)))
        level = level * jnp.repeat(steps, dims[dim] // parts).reshape([-1 if axis == dim else 1 for axis in range(len(dims))])
    return level


def centred(stream_key, extent, deviation, reach, pieces=(), kind=jnp.bfloat16):
    gain = shard_levels(stream_key, extent, pieces, -0.22, 0.18) if pieces else 1.0
    drawn = jax.random.normal(stream_key, extent, jnp.float32) * deviation * gain
    return jnp.minimum(jnp.maximum(drawn, -reach), reach).astype(kind)


def setup_inputs(seed: int = 0) -> dict:
    keys = jax.random.split(jax.random.key(seed), 4)
    return {
        "record": centred(keys[0], (TIME, 3, PTS), 1.0, 6.0, ((0, 8), (2, 4)), jnp.float32),
        "area_weight": jnp.clip(jnp.exp(math.log(5.0) - 3.218876 * jax.random.uniform(keys[1], (PTS,), jnp.float32) ** shard_levels(keys[1], (PTS,), ((0, 4),), -0.2, 0.2)), 0.2, 5.0),
        "freq_bins": draw_freq_bins(jax.random.fold_in(keys[3], 71), 0),
    }


def spectral_table(freq_bins):
    sample_index = jnp.arange(SAMPLES, dtype=jnp.int32)
    phase_steps = freq_bins[:, None] * sample_index[None, :] % SAMPLES
    angles = phase_steps.astype(jnp.float32) * (2.0 * math.pi / SAMPLES)
    window = 0.5 - 0.5 * jnp.cos(sample_index.astype(jnp.float32) * (2.0 * math.pi / SAMPLES))
    window = window / jnp.sqrt(jnp.sum(window * window))
    return jnp.stack([jnp.cos(angles), -jnp.sin(angles)], axis=1) * window

def complex_form(partial_value):
    bin_count = partial_value.shape[0]
    half_size = partial_value.shape[1] // 2
    blocked = partial_value.reshape(bin_count, half_size, 2, half_size, 2)
    real_part = blocked[:, :, 0, :, 0] + blocked[:, :, 1, :, 1]
    imag_part = blocked[:, :, 0, :, 1] - blocked[:, :, 1, :, 0]
    upper_rows = jnp.stack([real_part, imag_part], axis=-1)
    lower_rows = jnp.stack([-imag_part, real_part], axis=-1)
    assembled = jnp.stack([upper_rows, lower_rows], axis=2)
    return assembled.reshape(bin_count, 2 * half_size, 2 * half_size)

def reference(record, area_weight, freq_bins):
    transform = spectral_table(freq_bins)
    groups = record.reshape(BLOCKS, HOP, 3, PTS)
    later_groups = jnp.roll(groups, -1, axis=0)
    scaled_weight = area_weight / (3 * PTS)

    def single_bin(table_row):
        leading = jnp.einsum('qn,bncp->bqcp', table_row[:, :HOP], groups, precision=lax.Precision.HIGHEST)
        trailing = jnp.einsum('qn,bncp->bqcp', table_row[:, HOP:], later_groups, precision=lax.Precision.HIGHEST)
        spectra = leading + trailing
        flattened = spectra.reshape(2 * BLOCKS, 3 * PTS)
        weighted = (spectra * scaled_weight).reshape(2 * BLOCKS, 3 * PTS)
        partial_value = jnp.dot(weighted.astype(jnp.float32), flattened.T.astype(jnp.float32), precision=lax.Precision.HIGHEST, preferred_element_type=jnp.float32)
        gram = complex_form(partial_value[None])[0]
        lower_factor = jnp.linalg.cholesky(gram)
        solved = lax.linalg.triangular_solve(lower_factor, flattened, left_side=True, lower=True)
        upper_factor = lower_factor.T.reshape(BLOCKS, 2, BLOCKS, 2)
        factor = jnp.stack([upper_factor[:, 0, :, 0], upper_factor[:, 0, :, 1]])
        return (solved.reshape(BLOCKS, 2, 3, PTS).astype(jnp.bfloat16), factor)
    modes, factor = lax.map(single_bin, transform)
    return (modes, factor)
```

```python
import functools
import math

import jax
import jax.numpy as jnp
from jax import lax
from jax.experimental import pallas as pl
from jax.experimental.pallas import tpu as pltpu
from jax.sharding import PartitionSpec as P

PTS = 16384
SAMPLES = 128
HALF = SAMPLES // 2
COMPS = 3
CUTS = 2
F32, BF16 = jnp.float32, jnp.bfloat16
MESH = pl.DeviceIdType.MESH


def split3(value):
    first = value.astype(BF16)
    rest = value - first.astype(F32)
    second = rest.astype(BF16)
    third = (rest - second.astype(F32)).astype(BF16)
    return first, second, third


def turn(steps):
    shifted = (steps + 16) & 127
    quarter = shifted >> 5
    small = ((shifted & 31) - 16).astype(F32) * (math.pi / 64.0)
    square = small * small
    sine = small * (1.0 + square * (-1.0 / 6 + square * (1.0 / 120 + square * (-1.0 / 5040 + square * (1.0 / 362880)))))
    cosine = 1.0 + square * (-0.5 + square * (1.0 / 24 + square * (-1.0 / 720 + square * (1.0 / 40320 - square * (1.0 / 3628800)))))
    odd = (quarter & 1) == 1
    cos_size, sin_size = jnp.where(odd, sine, cosine), jnp.where(odd, cosine, sine)
    cos_value = jnp.where((quarter == 1) | (quarter == 2), -cos_size, cos_size)
    sin_value = jnp.where(quarter >= 2, -sin_size, sin_size)
    return cos_value, sin_value


def build_table(bins_ref, pairs, me_x):
    rows = 8 * pairs
    row = lax.broadcasted_iota(jnp.int32, (rows, HALF), 0)
    sample = lax.broadcasted_iota(jnp.int32, (rows, HALF), 1)
    bin_value = jnp.zeros((rows, HALF), jnp.int32)
    for group in range(2):
        parity = me_x if group == 0 else 1 - me_x
        for other in range(pairs):
            value = bins_ref[2 * other + parity]
            here = ((row // (4 * pairs)) == group) & (((row % (2 * pairs)) // 2) == other)
            bin_value = jnp.where(here, value, bin_value)
    trailing = ((row // (2 * pairs)) + me_x) & 1
    sample = sample + HALF * trailing
    cosine, sine = turn((bin_value * sample) & 127)
    window_cos, _ = turn(sample)
    window = (0.5 - 0.5 * window_cos) * (1.0 / math.sqrt(48.0))
    return jnp.where((row & 1) == 0, cosine, -sine) * window


def kernel(pairs, spaces, bins_ref, weight_ref, record_ref, modes_ref, factor_ref,
           rec, wbuf, xsend, xrecv, abuf, zsend, zrecv, split, gsend, grecv,
           in_sem, w_sem, x_ssem, x_rsem, e_ssem, e_rsem, l_ssem, l_rsem, g_ssem, g_rsem):
    blocks = 2 * pairs
    two = 2 * blocks
    points = record_ref.shape[2]
    cols = points // CUTS
    chunks = COMPS * CUTS
    me = lax.axis_index("freq")
    my_s = lax.axis_index("space")
    me_x = lax.rem(me, 2)
    me_z = lax.div(me, 2)
    partner = me + 1 - 2 * me_x
    early = 2 - 2 * me_x
    late = 2 * me_x

    barrier = pltpu.get_barrier_semaphore()
    pl.semaphore_signal(barrier, inc=1, device_id=(partner, my_s), device_id_type=MESH)
    for step in range(1, pairs):
        pl.semaphore_signal(barrier, inc=1, device_id=(lax.rem(me + 2 * step, blocks), my_s), device_id_type=MESH)
    for step in range(1, spaces):
        pl.semaphore_signal(barrier, inc=1, device_id=(me, lax.rem(my_s + step, spaces)), device_id_type=MESH)

    loads = []
    for k in range(chunks):
        load = pltpu.make_async_copy(
            record_ref.at[k // CUTS, :, pl.ds((k % CUTS) * cols, cols)], rec.at[k], in_sem.at[k])
        load.start()
        loads.append(load)
    w_load = pltpu.make_async_copy(weight_ref, wbuf, w_sem)
    w_load.start()

    t1, t2, t3 = split3(build_table(bins_ref, pairs, me_x))
    table_a = jnp.concatenate([t1, t2, t1], axis=1)
    table_b = jnp.concatenate([t2, t3, t1], axis=1)

    pl.semaphore_wait(barrier, 1 + (pairs - 1) + (spaces - 1))

    sends = []
    xcopies = []
    for k in range(chunks):
        loads[k].wait()
        r1, r2, r3 = split3(rec[k])
        part = jnp.dot(table_a, jnp.concatenate([r1, r1, r2], axis=0), preferred_element_type=F32) + jnp.dot(
            table_b, jnp.concatenate([r2, r1, r3], axis=0), preferred_element_type=F32)
        xsend[k] = part[4 * pairs:]
        copy = pltpu.make_async_remote_copy(
            src_ref=xsend.at[k], dst_ref=xrecv.at[k], send_sem=x_ssem.at[k], recv_sem=x_rsem.at[k],
            device_id=(partner, my_s), device_id_type=MESH)
        copy.start()
        xcopies.append(copy)
        abuf[k] = part[:2 * pairs]
        for other in range(pairs):
            zsend[k, other, early] = part[2 * pairs + 2 * other:2 * pairs + 2 * other + 2]
        for step in range(1, pairs):
            to = lax.rem(me_z + step, pairs)
            copy = pltpu.make_async_remote_copy(
                src_ref=zsend.at[k, to, early], dst_ref=zrecv.at[k, me_z, early],
                send_sem=e_ssem.at[k, step], recv_sem=e_rsem.at[k, step],
                device_id=(2 * to + me_x, my_s), device_id_type=MESH)
            copy.start()
            sends.append(copy)

    for k in range(chunks):
        xcopies[k].wait_recv()
        total = abuf[k] + xrecv[k, :2 * pairs]
        passed = xrecv[k, 2 * pairs:]
        for other in range(pairs):
            zsend[k, other, 1] = total[2 * other:2 * other + 2]
            zsend[k, other, late] = passed[2 * other:2 * other + 2]
        for step in range(1, pairs):
            to = lax.rem(me_z + step, pairs)
            copy = pltpu.make_async_remote_copy(
                src_ref=zsend.at[k, to, pl.ds(me_x, 2)], dst_ref=zrecv.at[k, me_z, pl.ds(me_x, 2)],
                send_sem=l_ssem.at[k, step], recv_sem=l_rsem.at[k, step],
                device_id=(2 * to + me_x, my_s), device_id_type=MESH)
            copy.start()
            sends.append(copy)
        zrecv[k, me_z] = zsend[k, me_z]

    w_load.wait()
    gram = None
    per = 2 * (pairs - 1)
    for k in range(chunks):
        comp, cut = k // CUTS, k % CUTS
        for step in range(1, pairs):
            sends[k * (pairs - 1) + step - 1].wait_recv()
            sends[(chunks + k) * (pairs - 1) + step - 1].wait_recv()
        pieces = []
        for z in range(pairs):
            pieces.append(zrecv[k, z, 1])
            pieces.append(zrecv[k, z, 0] + zrecv[k, (z + 1) % pairs, 2])
        value = jnp.concatenate([piece[0:1] for piece in pieces] + [piece[1:2] for piece in pieces], axis=0)
        parts = jnp.concatenate(split3(value), axis=0)
        split[comp, :, cut * cols:(cut + 1) * cols] = parts
        weighted = value * (wbuf[:, cut * cols:(cut + 1) * cols] * (1.0 / (COMPS * PTS)))
        wparts = jnp.concatenate(split3(weighted), axis=0)
        product = lax.dot_general(wparts, parts, (((1,), (1,)), ((), ())), preferred_element_type=F32)
        gram = product if gram is None else gram + product
    small = None
    for i in (2, 1, 0):
        for j in (2, 1, 0):
            term = gram[i * two:(i + 1) * two, j * two:(j + 1) * two]
            small = term if small is None else small + term
    real = small[:blocks, :blocks] + small[blocks:, blocks:]
    imag = small[:blocks, blocks:] - small[blocks:, :blocks]
    gsend[...] = jnp.concatenate([real, imag] + [jnp.zeros((blocks, gsend.shape[1] - two), F32)] * (gsend.shape[1] > two), axis=1)
    gcopies = []
    for step in range(1, spaces):
        copy = pltpu.make_async_remote_copy(
            src_ref=gsend, dst_ref=grecv.at[my_s], send_sem=g_ssem.at[step], recv_sem=g_rsem.at[step],
            device_id=(me, lax.rem(my_s + step, spaces)), device_id_type=MESH)
        copy.start()
        gcopies.append(copy)
    grecv[my_s] = gsend[...]
    for copy in gcopies:
        copy.wait_recv()
    whole = grecv[0]
    for s in range(1, spaces):
        whole = whole + grecv[s]

    row = lax.broadcasted_iota(jnp.int32, (blocks, two), 0)
    lane = lax.broadcasted_iota(jnp.int32, (blocks, two), 1)
    unit = (lane == row + blocks).astype(F32)
    left = lane < blocks
    re = jnp.where(left, whole[:, :two], unit)
    im = jnp.where(left, jnp.concatenate([whole[:, blocks:two], whole[:, :blocks]], axis=1), 0.0)
    for j in range(blocks - 1):
        inverse = 1.0 / re[j:j + 1, j:j + 1]
        row_re, row_im = re[j:j + 1] * inverse, im[j:j + 1] * inverse
        below = row > j
        col_re = jnp.where(below, re[:, j:j + 1], 0.0)
        col_im = jnp.where(below, im[:, j:j + 1], 0.0)
        re, im = re - (col_re * row_re - col_im * row_im), im - (col_re * row_im + col_im * row_re)
    pivots = jnp.sum(jnp.where(lane == row, re, 0.0), axis=1, keepdims=True)
    scale = 1.0 / jnp.sqrt(pivots)
    re, im = re * scale, im * scale
    factor_ref[0] = jnp.where(lane >= row, re, 0.0)[:, :blocks]
    factor_ref[1] = jnp.where(lane > row, im, 0.0)[:, :blocks]
    wr, wi = re[:, blocks:], im[:, blocks:]
    upper = jnp.concatenate([wr, wi], axis=1)
    lower = jnp.concatenate([-wi, wr], axis=1)
    mixed = jnp.concatenate([src[b:b + 1] for b in range(blocks) for src in (upper, lower)], axis=0)
    m1, m2, m3 = split3(mixed)
    weights = jnp.concatenate([m1, m1, m2, m2, m1, m3], axis=1)
    for comp in range(COMPS):
        x1, x2, x3 = (split[comp, i * two:(i + 1) * two] for i in range(3))
        out = jnp.dot(weights, jnp.concatenate([x1, x2, x1, x2, x3, x1], axis=0), preferred_element_type=F32)
        modes_ref[comp] = out.astype(BF16)
    for copy in xcopies + sends + gcopies:
        copy.wait_send()


def solution(mesh):
    count, spaces = mesh.shape["freq"], mesh.shape["space"]
    pairs = count // 2

    def per_device(record, area_weight, freq_bins):
        points = record.shape[2]
        cols = points // CUTS
        chunks = COMPS * CUTS
        two = 2 * count
        lanes = max(128, two)
        dma = pltpu.SemaphoreType.DMA
        modes, factor = pl.pallas_call(
            functools.partial(kernel, pairs, spaces),
            out_shape=(
                jax.ShapeDtypeStruct((COMPS, two, points), BF16),
                jax.ShapeDtypeStruct((2, count, count), F32),
            ),
            in_specs=[
                pl.BlockSpec(memory_space=pltpu.SMEM),
                pl.BlockSpec(memory_space=pl.ANY),
                pl.BlockSpec(memory_space=pl.ANY),
            ],
            out_specs=(pl.BlockSpec(memory_space=pltpu.VMEM), pl.BlockSpec(memory_space=pltpu.VMEM)),
            scratch_shapes=[
                pltpu.VMEM((chunks, HALF, cols), F32),
                pltpu.VMEM((1, points), F32),
                pltpu.VMEM((chunks, 4 * pairs, cols), F32),
                pltpu.VMEM((chunks, 4 * pairs, cols), F32),
                pltpu.VMEM((chunks, 2 * pairs, cols), F32),
                pltpu.VMEM((chunks, pairs, 3, 2, cols), F32),
                pltpu.VMEM((chunks, pairs, 3, 2, cols), F32),
                pltpu.VMEM((COMPS, 3 * two, points), BF16),
                pltpu.VMEM((count, lanes), F32),
                pltpu.VMEM((spaces, count, lanes), F32),
                dma((chunks,)), dma,
                dma((chunks,)), dma((chunks,)),
                dma((chunks, pairs)), dma((chunks, pairs)),
                dma((chunks, pairs)), dma((chunks, pairs)),
                dma((spaces,)), dma((spaces,)),
            ],
            compiler_params=pltpu.CompilerParams(
                collective_id=0, has_side_effects=True, vmem_limit_bytes=56 * 1024 * 1024),
        )(freq_bins, area_weight.reshape(1, points), record.transpose(1, 0, 2))
        modes = modes.reshape(COMPS, count, 2, points).transpose(1, 2, 0, 3)
        return modes[None], factor[None]

    return jax.shard_map(
        per_device,
        mesh=mesh,
        in_specs=(P("freq", None, "space"), P("space"), P()),
        out_specs=(P("freq", None, None, None, "space"), P("freq", None, None, None)),
        check_vma=False,
    )
```

```python
import functools
import math

import jax
import jax.numpy as jnp
from jax import lax
from jax.experimental import pallas as pl
from jax.experimental.pallas import tpu as pltpu
from jax.sharding import PartitionSpec as P

PTS = 16384
SAMPLES = 128
HALF = SAMPLES // 2
COMPS = 3
CUTS = 2
F32, BF16 = jnp.float32, jnp.bfloat16
MESH = pl.DeviceIdType.MESH


def split3(value):
    first = value.astype(BF16)
    rest = value - first.astype(F32)
    second = rest.astype(BF16)
    third = (rest - second.astype(F32)).astype(BF16)
    return first, second, third


def turn(steps):
    shifted = (steps + 16) & 127
    quarter = shifted >> 5
    small = ((shifted & 31) - 16).astype(F32) * (math.pi / 64.0)
    square = small * small
    sine = small * (1.0 + square * (-1.0 / 6 + square * (1.0 / 120 + square * (-1.0 / 5040 + square * (1.0 / 362880)))))
    cosine = 1.0 + square * (-0.5 + square * (1.0 / 24 + square * (-1.0 / 720 + square * (1.0 / 40320 - square * (1.0 / 3628800)))))
    odd = (quarter & 1) == 1
    cos_size, sin_size = jnp.where(odd, sine, cosine), jnp.where(odd, cosine, sine)
    cos_value = jnp.where((quarter == 1) | (quarter == 2), -cos_size, cos_size)
    sin_value = jnp.where(quarter >= 2, -sin_size, sin_size)
    return cos_value, sin_value


def build_table(bins_ref, pairs, me_x):
    rows = 8 * pairs
    row = lax.broadcasted_iota(jnp.int32, (rows, HALF), 0)
    sample = lax.broadcasted_iota(jnp.int32, (rows, HALF), 1)
    bin_value = jnp.zeros((rows, HALF), jnp.int32)
    for group in range(2):
        parity = me_x if group == 0 else 1 - me_x
        for other in range(pairs):
            value = bins_ref[2 * other + parity]
            here = ((row // (4 * pairs)) == group) & (((row % (2 * pairs)) // 2) == other)
            bin_value = jnp.where(here, value, bin_value)
    trailing = ((row // (2 * pairs)) + me_x) & 1
    sample = sample + HALF * trailing
    cosine, sine = turn((bin_value * sample) & 127)
    window_cos, _ = turn(sample)
    window = (0.5 - 0.5 * window_cos) * (1.0 / math.sqrt(48.0))
    return jnp.where((row & 1) == 0, cosine, -sine) * window


def kernel(pairs, spaces, bins_ref, weight_ref, record_ref, split_ref, gram_ref,
           rec, wbuf, xsend, xrecv, abuf, zsend, zrecv, split, gsend, grecv,
           in_sem, w_sem, out_sem, x_ssem, x_rsem, e_ssem, e_rsem, l_ssem, l_rsem, g_ssem, g_rsem):
    blocks = 2 * pairs
    two = 2 * blocks
    points = record_ref.shape[2]
    cols = points // CUTS
    chunks = COMPS * CUTS
    me = lax.axis_index("freq")
    my_s = lax.axis_index("space")
    me_x = lax.rem(me, 2)
    me_z = lax.div(me, 2)
    partner = me + 1 - 2 * me_x
    early = 2 - 2 * me_x
    late = 2 * me_x

    barrier = pltpu.get_barrier_semaphore()
    pl.semaphore_signal(barrier, inc=1, device_id=(partner, my_s), device_id_type=MESH)
    for step in range(1, pairs):
        pl.semaphore_signal(barrier, inc=1, device_id=(lax.rem(me + 2 * step, blocks), my_s), device_id_type=MESH)
    for step in range(1, spaces):
        pl.semaphore_signal(barrier, inc=1, device_id=(me, lax.rem(my_s + step, spaces)), device_id_type=MESH)

    loads = []
    for k in range(chunks):
        load = pltpu.make_async_copy(
            record_ref.at[k // CUTS, :, pl.ds((k % CUTS) * cols, cols)], rec.at[k], in_sem.at[k])
        load.start()
        loads.append(load)
    w_load = pltpu.make_async_copy(weight_ref, wbuf, w_sem)
    w_load.start()

    t1, t2, t3 = split3(build_table(bins_ref, pairs, me_x))
    table_a = jnp.concatenate([t1, t2, t1], axis=1)
    table_b = jnp.concatenate([t2, t3, t1], axis=1)

    pl.semaphore_wait(barrier, 1 + (pairs - 1) + (spaces - 1))

    sends = []
    xcopies = []
    for k in range(chunks):
        loads[k].wait()
        r1, r2, r3 = split3(rec[k])
        part = jnp.dot(table_a, jnp.concatenate([r1, r1, r2], axis=0), preferred_element_type=F32) + jnp.dot(
            table_b, jnp.concatenate([r2, r1, r3], axis=0), preferred_element_type=F32)
        xsend[k] = part[4 * pairs:]
        copy = pltpu.make_async_remote_copy(
            src_ref=xsend.at[k], dst_ref=xrecv.at[k], send_sem=x_ssem.at[k], recv_sem=x_rsem.at[k],
            device_id=(partner, my_s), device_id_type=MESH)
        copy.start()
        xcopies.append(copy)
        abuf[k] = part[:2 * pairs]
        for other in range(pairs):
            zsend[k, other, early] = part[2 * pairs + 2 * other:2 * pairs + 2 * other + 2]
        for step in range(1, pairs):
            to = lax.rem(me_z + step, pairs)
            copy = pltpu.make_async_remote_copy(
                src_ref=zsend.at[k, to, early], dst_ref=zrecv.at[k, me_z, early],
                send_sem=e_ssem.at[k, step], recv_sem=e_rsem.at[k, step],
                device_id=(2 * to + me_x, my_s), device_id_type=MESH)
            copy.start()
            sends.append(copy)

    for k in range(chunks):
        xcopies[k].wait_recv()
        total = abuf[k] + xrecv[k, :2 * pairs]
        passed = xrecv[k, 2 * pairs:]
        for other in range(pairs):
            zsend[k, other, 1] = total[2 * other:2 * other + 2]
            zsend[k, other, late] = passed[2 * other:2 * other + 2]
        for step in range(1, pairs):
            to = lax.rem(me_z + step, pairs)
            copy = pltpu.make_async_remote_copy(
                src_ref=zsend.at[k, to, pl.ds(me_x, 2)], dst_ref=zrecv.at[k, me_z, pl.ds(me_x, 2)],
                send_sem=l_ssem.at[k, step], recv_sem=l_rsem.at[k, step],
                device_id=(2 * to + me_x, my_s), device_id_type=MESH)
            copy.start()
            sends.append(copy)
        zrecv[k, me_z] = zsend[k, me_z]

    w_load.wait()
    gram = None
    stores = []
    per = 2 * (pairs - 1)
    for k in range(chunks):
        comp, cut = k // CUTS, k % CUTS
        for step in range(1, pairs):
            sends[k * (pairs - 1) + step - 1].wait_recv()
            sends[(chunks + k) * (pairs - 1) + step - 1].wait_recv()
        pieces = []
        for z in range(pairs):
            pieces.append(zrecv[k, z, 1])
            pieces.append(zrecv[k, z, 0] + zrecv[k, (z + 1) % pairs, 2])
        value = jnp.concatenate([piece[0:1] for piece in pieces] + [piece[1:2] for piece in pieces], axis=0)
        parts = jnp.concatenate(split3(value), axis=0)
        split[k] = parts
        store = pltpu.make_async_copy(
            split.at[k], split_ref.at[comp, :, pl.ds(cut * cols, cols)], out_sem.at[k])
        store.start()
        stores.append(store)
        weighted = value * (wbuf[:, cut * cols:(cut + 1) * cols] * (1.0 / (COMPS * PTS)))
        wparts = jnp.concatenate(split3(weighted), axis=0)
        product = lax.dot_general(wparts, parts, (((1,), (1,)), ((), ())), preferred_element_type=F32)
        gram = product if gram is None else gram + product
    small = None
    for i in (2, 1, 0):
        for j in (2, 1, 0):
            term = gram[i * two:(i + 1) * two, j * two:(j + 1) * two]
            small = term if small is None else small + term
    real = small[:blocks, :blocks] + small[blocks:, blocks:]
    imag = small[:blocks, blocks:] - small[blocks:, :blocks]
    gsend[...] = jnp.concatenate([real, imag] + [jnp.zeros((blocks, gsend.shape[1] - two), F32)] * (gsend.shape[1] > two), axis=1)
    gcopies = []
    for step in range(1, spaces):
        copy = pltpu.make_async_remote_copy(
            src_ref=gsend, dst_ref=grecv.at[my_s], send_sem=g_ssem.at[step], recv_sem=g_rsem.at[step],
            device_id=(me, lax.rem(my_s + step, spaces)), device_id_type=MESH)
        copy.start()
        gcopies.append(copy)
    grecv[my_s] = gsend[...]
    for copy in gcopies:
        copy.wait_recv()
    whole = grecv[0]
    for s in range(1, spaces):
        whole = whole + grecv[s]

    gram_ref[...] = whole
    for copy in stores:
        copy.wait()
    for copy in xcopies + sends + gcopies:
        copy.wait_send()


def finish(blocks, gram_ref, split_ref, modes_ref, factor_ref, held, sem):
    two = 2 * blocks
    loads = []
    for comp in range(COMPS):
        load = pltpu.make_async_copy(split_ref.at[comp], held.at[comp], sem.at[comp])
        load.start()
        loads.append(load)
    whole = gram_ref[...]
    row = lax.broadcasted_iota(jnp.int32, (blocks, two), 0)
    lane = lax.broadcasted_iota(jnp.int32, (blocks, two), 1)
    unit = (lane == row + blocks).astype(F32)
    left = lane < blocks
    re = jnp.where(left, whole[:, :two], unit)
    im = jnp.where(left, jnp.concatenate([whole[:, blocks:two], whole[:, :blocks]], axis=1), 0.0)
    for j in range(blocks - 1):
        inverse = 1.0 / re[j:j + 1, j:j + 1]
        row_re, row_im = re[j:j + 1] * inverse, im[j:j + 1] * inverse
        below = row > j
        col_re = jnp.where(below, re[:, j:j + 1], 0.0)
        col_im = jnp.where(below, im[:, j:j + 1], 0.0)
        re, im = re - (col_re * row_re - col_im * row_im), im - (col_re * row_im + col_im * row_re)
    pivots = jnp.sum(jnp.where(lane == row, re, 0.0), axis=1, keepdims=True)
    scale = 1.0 / jnp.sqrt(pivots)
    re, im = re * scale, im * scale
    factor_ref[0] = jnp.where(lane >= row, re, 0.0)[:, :blocks]
    factor_ref[1] = jnp.where(lane > row, im, 0.0)[:, :blocks]
    wr, wi = re[:, blocks:], im[:, blocks:]
    upper = jnp.concatenate([wr, wi], axis=1)
    lower = jnp.concatenate([-wi, wr], axis=1)
    mixed = jnp.concatenate([src[b:b + 1] for b in range(blocks) for src in (upper, lower)], axis=0)
    m1, m2, m3 = split3(mixed)
    weights = jnp.concatenate([m1, m1, m2, m2, m1, m3], axis=1)
    for comp in range(COMPS):
        loads[comp].wait()
        x1, x2, x3 = (held[comp, i * two:(i + 1) * two] for i in range(3))
        out = jnp.dot(weights, jnp.concatenate([x1, x2, x1, x2, x3, x1], axis=0), preferred_element_type=F32)
        for b in range(blocks):
            modes_ref[b, comp] = out[2 * b:2 * b + 2].astype(BF16)


def solution(mesh):
    count, spaces = mesh.shape["freq"], mesh.shape["space"]
    pairs = count // 2

    def per_device(record, area_weight, freq_bins):
        points = record.shape[2]
        cols = points // CUTS
        chunks = COMPS * CUTS
        two = 2 * count
        lanes = max(128, two)
        dma = pltpu.SemaphoreType.DMA
        split, gram = pl.pallas_call(
            functools.partial(kernel, pairs, spaces),
            out_shape=(
                jax.ShapeDtypeStruct((COMPS, 3 * two, points), BF16),
                jax.ShapeDtypeStruct((count, lanes), F32),
            ),
            in_specs=[
                pl.BlockSpec(memory_space=pltpu.SMEM),
                pl.BlockSpec(memory_space=pl.ANY),
                pl.BlockSpec(memory_space=pl.ANY),
            ],
            out_specs=(pl.BlockSpec(memory_space=pl.ANY), pl.BlockSpec(memory_space=pltpu.VMEM)),
            scratch_shapes=[
                pltpu.VMEM((chunks, HALF, cols), F32),
                pltpu.VMEM((1, points), F32),
                pltpu.VMEM((chunks, 4 * pairs, cols), F32),
                pltpu.VMEM((chunks, 4 * pairs, cols), F32),
                pltpu.VMEM((chunks, 2 * pairs, cols), F32),
                pltpu.VMEM((chunks, pairs, 3, 2, cols), F32),
                pltpu.VMEM((chunks, pairs, 3, 2, cols), F32),
                pltpu.VMEM((chunks, 3 * two, cols), BF16),
                pltpu.VMEM((count, lanes), F32),
                pltpu.VMEM((spaces, count, lanes), F32),
                dma((chunks,)), dma, dma((chunks,)),
                dma((chunks,)), dma((chunks,)),
                dma((chunks, pairs)), dma((chunks, pairs)),
                dma((chunks, pairs)), dma((chunks, pairs)),
                dma((spaces,)), dma((spaces,)),
            ],
            compiler_params=pltpu.CompilerParams(
                collective_id=0, has_side_effects=True, vmem_limit_bytes=56 * 1024 * 1024),
        )(freq_bins, area_weight.reshape(1, points), record.transpose(1, 0, 2))
        modes, factor = pl.pallas_call(
            functools.partial(finish, count),
            out_shape=(
                jax.ShapeDtypeStruct((count, COMPS, 2, points), BF16),
                jax.ShapeDtypeStruct((2, count, count), F32),
            ),
            in_specs=[pl.BlockSpec(memory_space=pltpu.VMEM), pl.BlockSpec(memory_space=pl.ANY)],
            out_specs=(pl.BlockSpec(memory_space=pltpu.VMEM), pl.BlockSpec(memory_space=pltpu.VMEM)),
            scratch_shapes=[pltpu.VMEM((COMPS, 3 * two, points), BF16), dma((COMPS,))],
            compiler_params=pltpu.CompilerParams(vmem_limit_bytes=56 * 1024 * 1024),
        )(gram, split)
        return modes.transpose(0, 2, 1, 3)[None], factor[None]

    return jax.shard_map(
        per_device,
        mesh=mesh,
        in_specs=(P("freq", None, "space"), P("space"), P()),
        out_specs=(P("freq", None, None, None, "space"), P("freq", None, None, None)),
        check_vma=False,
    )
```

```python
import functools
import math

import jax
import jax.numpy as jnp
from jax import lax
from jax.experimental import pallas as pl
from jax.experimental.pallas import tpu as pltpu
from jax.sharding import PartitionSpec as P

PTS = 16384
SAMPLES = 128
HALF = SAMPLES // 2
COMPS = 3
CUTS = 2
F32, BF16 = jnp.float32, jnp.bfloat16
MESH = pl.DeviceIdType.MESH


def split3(value):
    first = value.astype(BF16)
    rest = value - first.astype(F32)
    second = rest.astype(BF16)
    third = (rest - second.astype(F32)).astype(BF16)
    return first, second, third


def turn(steps):
    shifted = (steps + 16) & 127
    quarter = shifted >> 5
    small = ((shifted & 31) - 16).astype(F32) * (math.pi / 64.0)
    square = small * small
    sine = small * (1.0 + square * (-1.0 / 6 + square * (1.0 / 120 + square * (-1.0 / 5040 + square * (1.0 / 362880)))))
    cosine = 1.0 + square * (-0.5 + square * (1.0 / 24 + square * (-1.0 / 720 + square * (1.0 / 40320 - square * (1.0 / 3628800)))))
    odd = (quarter & 1) == 1
    cos_size, sin_size = jnp.where(odd, sine, cosine), jnp.where(odd, cosine, sine)
    cos_value = jnp.where((quarter == 1) | (quarter == 2), -cos_size, cos_size)
    sin_value = jnp.where(quarter >= 2, -sin_size, sin_size)
    return cos_value, sin_value


def build_table(bins_ref, pairs, me_x):
    rows = 8 * pairs
    row = lax.broadcasted_iota(jnp.int32, (rows, HALF), 0)
    sample = lax.broadcasted_iota(jnp.int32, (rows, HALF), 1)
    bin_value = jnp.zeros((rows, HALF), jnp.int32)
    for group in range(2):
        parity = me_x if group == 0 else 1 - me_x
        for other in range(pairs):
            value = bins_ref[2 * other + parity]
            here = ((row // (4 * pairs)) == group) & (((row % (2 * pairs)) // 2) == other)
            bin_value = jnp.where(here, value, bin_value)
    trailing = ((row // (2 * pairs)) + me_x) & 1
    sample = sample + HALF * trailing
    cosine, sine = turn((bin_value * sample) & 127)
    window_cos, _ = turn(sample)
    window = (0.5 - 0.5 * window_cos) * (1.0 / math.sqrt(48.0))
    return jnp.where((row & 1) == 0, cosine, -sine) * window


def kernel(pairs, spaces, bins_ref, weight_ref, record_ref, split_ref, gram_ref,
           rec, wbuf, xsend, xrecv, abuf, zsend, zrecv, split, gsend, grecv,
           in_sem, w_sem, out_sem, x_ssem, x_rsem, e_ssem, e_rsem, l_ssem, l_rsem, g_ssem, g_rsem):
    blocks = 2 * pairs
    two = 2 * blocks
    points = record_ref.shape[2]
    cols = points // CUTS
    chunks = COMPS * CUTS
    me = lax.axis_index("freq")
    my_s = lax.axis_index("space")
    me_x = lax.rem(me, 2)
    me_z = lax.div(me, 2)
    partner = me + 1 - 2 * me_x
    early = 2 - 2 * me_x
    late = 2 * me_x

    barrier = pltpu.get_barrier_semaphore()
    pl.semaphore_signal(barrier, inc=1, device_id=(partner, my_s), device_id_type=MESH)
    for step in range(1, pairs):
        pl.semaphore_signal(barrier, inc=1, device_id=(lax.rem(me + 2 * step, blocks), my_s), device_id_type=MESH)
    for step in range(1, spaces):
        pl.semaphore_signal(barrier, inc=1, device_id=(me, lax.rem(my_s + step, spaces)), device_id_type=MESH)

    loads = []
    for k in range(chunks):
        load = pltpu.make_async_copy(
            record_ref.at[k // CUTS, :, pl.ds((k % CUTS) * cols, cols)], rec.at[k], in_sem.at[k])
        load.start()
        loads.append(load)
    w_load = pltpu.make_async_copy(weight_ref, wbuf, w_sem)
    w_load.start()

    t1, t2, t3 = split3(build_table(bins_ref, pairs, me_x))
    table_a = jnp.concatenate([t1, t2, t1], axis=1)
    table_b = jnp.concatenate([t2, t3, t1], axis=1)

    pl.semaphore_wait(barrier, 1 + (pairs - 1) + (spaces - 1))

    sends = []
    xcopies = []
    for k in range(chunks):
        loads[k].wait()
        r1, r2, r3 = split3(rec[k])
        part = jnp.dot(table_a, jnp.concatenate([r1, r1, r2], axis=0), preferred_element_type=F32) + jnp.dot(
            table_b, jnp.concatenate([r2, r1, r3], axis=0), preferred_element_type=F32)
        xsend[k] = part[4 * pairs:]
        copy = pltpu.make_async_remote_copy(
            src_ref=xsend.at[k], dst_ref=xrecv.at[k], send_sem=x_ssem.at[k], recv_sem=x_rsem.at[k],
            device_id=(partner, my_s), device_id_type=MESH)
        copy.start()
        xcopies.append(copy)
        abuf[k] = part[:2 * pairs]
        for other in range(pairs):
            zsend[k, other, early] = part[2 * pairs + 2 * other:2 * pairs + 2 * other + 2]
        for step in range(1, pairs):
            to = lax.rem(me_z + step, pairs)
            copy = pltpu.make_async_remote_copy(
                src_ref=zsend.at[k, to, early], dst_ref=zrecv.at[k, me_z, early],
                send_sem=e_ssem.at[k, step], recv_sem=e_rsem.at[k, step],
                device_id=(2 * to + me_x, my_s), device_id_type=MESH)
            copy.start()
            sends.append(copy)

    for k in range(chunks):
        xcopies[k].wait_recv()
        total = abuf[k] + xrecv[k, :2 * pairs]
        passed = xrecv[k, 2 * pairs:]
        for other in range(pairs):
            zsend[k, other, 1] = total[2 * other:2 * other + 2]
            zsend[k, other, late] = passed[2 * other:2 * other + 2]
        for step in range(1, pairs):
            to = lax.rem(me_z + step, pairs)
            copy = pltpu.make_async_remote_copy(
                src_ref=zsend.at[k, to, pl.ds(me_x, 2)], dst_ref=zrecv.at[k, me_z, pl.ds(me_x, 2)],
                send_sem=l_ssem.at[k, step], recv_sem=l_rsem.at[k, step],
                device_id=(2 * to + me_x, my_s), device_id_type=MESH)
            copy.start()
            sends.append(copy)
        zrecv[k, me_z] = zsend[k, me_z]

    w_load.wait()
    gram = None
    stores = []
    per = 2 * (pairs - 1)
    for k in range(chunks):
        comp, cut = k // CUTS, k % CUTS
        for step in range(1, pairs):
            sends[k * (pairs - 1) + step - 1].wait_recv()
            sends[(chunks + k) * (pairs - 1) + step - 1].wait_recv()
        pieces = []
        for z in range(pairs):
            pieces.append(zrecv[k, z, 1])
            pieces.append(zrecv[k, z, 0] + zrecv[k, (z + 1) % pairs, 2])
        value = jnp.concatenate([piece[0:1] for piece in pieces] + [piece[1:2] for piece in pieces], axis=0)
        parts = jnp.concatenate(split3(value), axis=0)
        split[k] = parts
        store = pltpu.make_async_copy(
            split.at[k], split_ref.at[comp, :, pl.ds(cut * cols, cols)], out_sem.at[k])
        store.start()
        stores.append(store)
        weighted = value * (wbuf[:, cut * cols:(cut + 1) * cols] * (1.0 / (COMPS * PTS)))
        wparts = jnp.concatenate(split3(weighted), axis=0)
        product = lax.dot_general(wparts, parts, (((1,), (1,)), ((), ())), preferred_element_type=F32)
        gram = product if gram is None else gram + product
    tall = (gram[2 * two:] + gram[two:2 * two]) + gram[:two]
    small = (tall[:, 2 * two:] + tall[:, two:2 * two]) + tall[:, :two]
    real = small[:blocks, :blocks] + small[blocks:, blocks:]
    imag = small[:blocks, blocks:] - small[blocks:, :blocks]
    gsend[...] = jnp.concatenate([real, imag] + [jnp.zeros((blocks, gsend.shape[1] - two), F32)] * (gsend.shape[1] > two), axis=1)
    gcopies = []
    for step in range(1, spaces):
        copy = pltpu.make_async_remote_copy(
            src_ref=gsend, dst_ref=grecv.at[my_s], send_sem=g_ssem.at[step], recv_sem=g_rsem.at[step],
            device_id=(me, lax.rem(my_s + step, spaces)), device_id_type=MESH)
        copy.start()
        gcopies.append(copy)
    grecv[my_s] = gsend[...]
    for copy in stores:
        copy.wait()
    for copy in xcopies + sends:
        copy.wait_send()
    for copy in gcopies:
        copy.wait_recv()
    whole = grecv[0]
    for s in range(1, spaces):
        whole = whole + grecv[s]

    gram_ref[...] = whole
    for copy in gcopies:
        copy.wait_send()


def finish(blocks, gram_ref, split_ref, modes_ref, factor_ref, held, sem):
    two = 2 * blocks
    loads = []
    for comp in range(COMPS):
        load = pltpu.make_async_copy(split_ref.at[comp], held.at[comp], sem.at[comp])
        load.start()
        loads.append(load)
    whole = gram_ref[...]
    row = lax.broadcasted_iota(jnp.int32, (blocks, two), 0)
    lane = lax.broadcasted_iota(jnp.int32, (blocks, two), 1)
    unit = (lane == row + blocks).astype(F32)
    left = lane < blocks
    re = jnp.where(left, whole[:, :two], unit)
    im = jnp.where(left, jnp.concatenate([whole[:, blocks:two], whole[:, :blocks]], axis=1), 0.0)
    for j in range(blocks - 1):
        inverse = 1.0 / re[j:j + 1, j:j + 1]
        row_re, row_im = re[j:j + 1] * inverse, im[j:j + 1] * inverse
        below = row > j
        col_re = jnp.where(below, re[:, j:j + 1], 0.0)
        col_im = jnp.where(below, im[:, j:j + 1], 0.0)
        re, im = re - (col_re * row_re - col_im * row_im), im - (col_re * row_im + col_im * row_re)
    pivots = jnp.sum(jnp.where(lane == row, re, 0.0), axis=1, keepdims=True)
    scale = 1.0 / jnp.sqrt(pivots)
    re, im = re * scale, im * scale
    factor_ref[0] = jnp.where(lane >= row, re, 0.0)[:, :blocks]
    factor_ref[1] = jnp.where(lane > row, im, 0.0)[:, :blocks]
    wr, wi = re[:, blocks:], im[:, blocks:]
    upper = jnp.concatenate([wr, wi], axis=1)
    lower = jnp.concatenate([-wi, wr], axis=1)
    mixed = jnp.concatenate([src[b:b + 1] for b in range(blocks) for src in (upper, lower)], axis=0)
    m1, m2, m3 = split3(mixed)
    weights = jnp.concatenate([m1, m1, m2, m2, m1, m3], axis=1)
    for comp in range(COMPS):
        loads[comp].wait()
        x1, x2, x3 = (held[comp, i * two:(i + 1) * two] for i in range(3))
        out = jnp.dot(weights, jnp.concatenate([x1, x2, x1, x2, x3, x1], axis=0), preferred_element_type=F32)
        for b in range(blocks):
            modes_ref[b, comp] = out[2 * b:2 * b + 2].astype(BF16)


def solution(mesh):
    count, spaces = mesh.shape["freq"], mesh.shape["space"]
    pairs = count // 2

    def per_device(record, area_weight, freq_bins):
        points = record.shape[2]
        cols = points // CUTS
        chunks = COMPS * CUTS
        two = 2 * count
        lanes = max(128, two)
        dma = pltpu.SemaphoreType.DMA
        split, gram = pl.pallas_call(
            functools.partial(kernel, pairs, spaces),
            out_shape=(
                jax.ShapeDtypeStruct((COMPS, 3 * two, points), BF16),
                jax.ShapeDtypeStruct((count, lanes), F32),
            ),
            in_specs=[
                pl.BlockSpec(memory_space=pltpu.SMEM),
                pl.BlockSpec(memory_space=pl.ANY),
                pl.BlockSpec(memory_space=pl.ANY),
            ],
            out_specs=(pl.BlockSpec(memory_space=pl.ANY), pl.BlockSpec(memory_space=pltpu.VMEM)),
            scratch_shapes=[
                pltpu.VMEM((chunks, HALF, cols), F32),
                pltpu.VMEM((1, points), F32),
                pltpu.VMEM((chunks, 4 * pairs, cols), F32),
                pltpu.VMEM((chunks, 4 * pairs, cols), F32),
                pltpu.VMEM((chunks, 2 * pairs, cols), F32),
                pltpu.VMEM((chunks, pairs, 3, 2, cols), F32),
                pltpu.VMEM((chunks, pairs, 3, 2, cols), F32),
                pltpu.VMEM((chunks, 3 * two, cols), BF16),
                pltpu.VMEM((count, lanes), F32),
                pltpu.VMEM((spaces, count, lanes), F32),
                dma((chunks,)), dma, dma((chunks,)),
                dma((chunks,)), dma((chunks,)),
                dma((chunks, pairs)), dma((chunks, pairs)),
                dma((chunks, pairs)), dma((chunks, pairs)),
                dma((spaces,)), dma((spaces,)),
            ],
            compiler_params=pltpu.CompilerParams(
                collective_id=0, has_side_effects=True, vmem_limit_bytes=56 * 1024 * 1024),
        )(freq_bins, area_weight.reshape(1, points), record.transpose(1, 0, 2))
        modes, factor = pl.pallas_call(
            functools.partial(finish, count),
            out_shape=(
                jax.ShapeDtypeStruct((count, COMPS, 2, points), BF16),
                jax.ShapeDtypeStruct((2, count, count), F32),
            ),
            in_specs=[pl.BlockSpec(memory_space=pltpu.VMEM), pl.BlockSpec(memory_space=pl.ANY)],
            out_specs=(pl.BlockSpec(memory_space=pltpu.VMEM), pl.BlockSpec(memory_space=pltpu.VMEM)),
            scratch_shapes=[pltpu.VMEM((COMPS, 3 * two, points), BF16), dma((COMPS,))],
            compiler_params=pltpu.CompilerParams(vmem_limit_bytes=56 * 1024 * 1024),
        )(gram, split)
        return modes.transpose(0, 2, 1, 3)[None], factor[None]

    return jax.shard_map(
        per_device,
        mesh=mesh,
        in_specs=(P("freq", None, "space"), P("space"), P()),
        out_specs=(P("freq", None, None, None, "space"), P("freq", None, None, None)),
        check_vma=False,
    )
```

```python
import functools
import math

import jax
import jax.numpy as jnp
from jax import lax
from jax.experimental import pallas as pl
from jax.experimental.pallas import tpu as pltpu
from jax.sharding import PartitionSpec as P

PTS = 16384
SAMPLES = 128
HALF = SAMPLES // 2
COMPS = 3
CUTS = 2
F32, BF16 = jnp.float32, jnp.bfloat16
MESH = pl.DeviceIdType.MESH


def split3(value):
    first = value.astype(BF16)
    rest = value - first.astype(F32)
    second = rest.astype(BF16)
    third = (rest - second.astype(F32)).astype(BF16)
    return first, second, third


def turn(steps):
    shifted = (steps + 16) & 127
    quarter = shifted >> 5
    small = ((shifted & 31) - 16).astype(F32) * (math.pi / 64.0)
    square = small * small
    sine = small * (1.0 + square * (-1.0 / 6 + square * (1.0 / 120 + square * (-1.0 / 5040 + square * (1.0 / 362880)))))
    cosine = 1.0 + square * (-0.5 + square * (1.0 / 24 + square * (-1.0 / 720 + square * (1.0 / 40320 - square * (1.0 / 3628800)))))
    odd = (quarter & 1) == 1
    cos_size, sin_size = jnp.where(odd, sine, cosine), jnp.where(odd, cosine, sine)
    cos_value = jnp.where((quarter == 1) | (quarter == 2), -cos_size, cos_size)
    sin_value = jnp.where(quarter >= 2, -sin_size, sin_size)
    return cos_value, sin_value


def build_table(bins_ref, pairs, me_x):
    rows = 8 * pairs
    row = lax.broadcasted_iota(jnp.int32, (rows, HALF), 0)
    sample = lax.broadcasted_iota(jnp.int32, (rows, HALF), 1)
    bin_value = jnp.zeros((rows, HALF), jnp.int32)
    for group in range(2):
        parity = me_x if group == 0 else 1 - me_x
        for other in range(pairs):
            value = bins_ref[2 * other + parity]
            here = ((row // (4 * pairs)) == group) & (((row % (2 * pairs)) // 2) == other)
            bin_value = jnp.where(here, value, bin_value)
    trailing = ((row // (2 * pairs)) + me_x) & 1
    sample = sample + HALF * trailing
    cosine, sine = turn((bin_value * sample) & 127)
    window_cos, _ = turn(sample)
    window = (0.5 - 0.5 * window_cos) * (1.0 / math.sqrt(48.0))
    return jnp.where((row & 1) == 0, cosine, -sine) * window


def kernel(pairs, spaces, bins_ref, weight_ref, record_ref, split_ref, gram_ref,
           rec, wbuf, xsend, xrecv, abuf, zsend, zrecv, split, gsend, grecv,
           in_sem, w_sem, out_sem, x_ssem, x_rsem, e_ssem, e_rsem, l_ssem, l_rsem, g_ssem, g_rsem):
    blocks = 2 * pairs
    two = 2 * blocks
    points = record_ref.shape[2]
    cols = points // CUTS
    chunks = COMPS * CUTS
    me = lax.axis_index("freq")
    my_s = lax.axis_index("space")
    me_x = lax.rem(me, 2)
    me_z = lax.div(me, 2)
    partner = me + 1 - 2 * me_x
    early = 2 - 2 * me_x
    late = 2 * me_x

    barrier = pltpu.get_barrier_semaphore()
    pl.semaphore_signal(barrier, inc=1, device_id=(partner, my_s), device_id_type=MESH)
    for step in range(1, pairs):
        pl.semaphore_signal(barrier, inc=1, device_id=(lax.rem(me + 2 * step, blocks), my_s), device_id_type=MESH)
    for step in range(1, spaces):
        pl.semaphore_signal(barrier, inc=1, device_id=(me, lax.rem(my_s + step, spaces)), device_id_type=MESH)

    loads = []
    for k in range(chunks):
        load = pltpu.make_async_copy(
            record_ref.at[k // CUTS, :, pl.ds((k % CUTS) * cols, cols)], rec.at[k], in_sem.at[k])
        load.start()
        loads.append(load)
    w_load = pltpu.make_async_copy(weight_ref, wbuf, w_sem)
    w_load.start()

    t1, t2, t3 = split3(build_table(bins_ref, pairs, me_x))
    table_a = jnp.concatenate([t1, t2, t1], axis=1)
    table_b = jnp.concatenate([t2, t3, t1], axis=1)

    pl.semaphore_wait(barrier, 1 + (pairs - 1) + (spaces - 1))

    sends = []
    xcopies = []
    for k in range(chunks):
        loads[k].wait()
        r1, r2, r3 = split3(rec[k])
        part = jnp.dot(table_a, jnp.concatenate([r1, r1, r2], axis=0), preferred_element_type=F32) + jnp.dot(
            table_b, jnp.concatenate([r2, r1, r3], axis=0), preferred_element_type=F32)
        xsend[k] = part[4 * pairs:]
        copy = pltpu.make_async_remote_copy(
            src_ref=xsend.at[k], dst_ref=xrecv.at[k], send_sem=x_ssem.at[k], recv_sem=x_rsem.at[k],
            device_id=(partner, my_s), device_id_type=MESH)
        copy.start()
        xcopies.append(copy)
        abuf[k] = part[:2 * pairs]
        for other in range(pairs):
            zsend[k, other, early] = part[2 * pairs + 2 * other:2 * pairs + 2 * other + 2]
        for step in sorted(range(1, pairs), key=lambda step: abs(step - pairs // 2)):
            to = lax.rem(me_z + step, pairs)
            copy = pltpu.make_async_remote_copy(
                src_ref=zsend.at[k, to, early], dst_ref=zrecv.at[k, me_z, early],
                send_sem=e_ssem.at[k, step], recv_sem=e_rsem.at[k, step],
                device_id=(2 * to + me_x, my_s), device_id_type=MESH)
            copy.start()
            sends.append(copy)

    for k in range(chunks):
        xcopies[k].wait_recv()
        total = abuf[k] + xrecv[k, :2 * pairs]
        passed = xrecv[k, 2 * pairs:]
        for other in range(pairs):
            zsend[k, other, 1] = total[2 * other:2 * other + 2]
            zsend[k, other, late] = passed[2 * other:2 * other + 2]
        for step in sorted(range(1, pairs), key=lambda step: abs(step - pairs // 2)):
            to = lax.rem(me_z + step, pairs)
            copy = pltpu.make_async_remote_copy(
                src_ref=zsend.at[k, to, pl.ds(me_x, 2)], dst_ref=zrecv.at[k, me_z, pl.ds(me_x, 2)],
                send_sem=l_ssem.at[k, step], recv_sem=l_rsem.at[k, step],
                device_id=(2 * to + me_x, my_s), device_id_type=MESH)
            copy.start()
            sends.append(copy)
        zrecv[k, me_z] = zsend[k, me_z]

    w_load.wait()
    gram = None
    stores = []
    per = 2 * (pairs - 1)
    for k in range(chunks):
        comp, cut = k // CUTS, k % CUTS
        for step in range(1, pairs):
            sends[k * (pairs - 1) + step - 1].wait_recv()
            sends[(chunks + k) * (pairs - 1) + step - 1].wait_recv()
        pieces = []
        for z in range(pairs):
            pieces.append(zrecv[k, z, 1])
            pieces.append(zrecv[k, z, 0] + zrecv[k, (z + 1) % pairs, 2])
        value = jnp.concatenate([piece[0:1] for piece in pieces] + [piece[1:2] for piece in pieces], axis=0)
        parts = jnp.concatenate(split3(value), axis=0)
        split[k] = parts
        store = pltpu.make_async_copy(
            split.at[k], split_ref.at[comp, :, pl.ds(cut * cols, cols)], out_sem.at[k])
        store.start()
        stores.append(store)
        weighted = value * (wbuf[:, cut * cols:(cut + 1) * cols] * (1.0 / (COMPS * PTS)))
        wparts = jnp.concatenate(split3(weighted), axis=0)
        product = lax.dot_general(wparts, parts, (((1,), (1,)), ((), ())), preferred_element_type=F32)
        gram = product if gram is None else gram + product
    tall = (gram[2 * two:] + gram[two:2 * two]) + gram[:two]
    small = (tall[:, 2 * two:] + tall[:, two:2 * two]) + tall[:, :two]
    real = small[:blocks, :blocks] + small[blocks:, blocks:]
    imag = small[:blocks, blocks:] - small[blocks:, :blocks]
    gsend[...] = jnp.concatenate([real, imag] + [jnp.zeros((blocks, gsend.shape[1] - two), F32)] * (gsend.shape[1] > two), axis=1)
    gcopies = []
    for step in range(1, spaces):
        copy = pltpu.make_async_remote_copy(
            src_ref=gsend, dst_ref=grecv.at[my_s], send_sem=g_ssem.at[step], recv_sem=g_rsem.at[step],
            device_id=(me, lax.rem(my_s + step, spaces)), device_id_type=MESH)
        copy.start()
        gcopies.append(copy)
    grecv[my_s] = gsend[...]
    for copy in stores:
        copy.wait()
    for copy in xcopies + sends:
        copy.wait_send()
    for copy in gcopies:
        copy.wait_recv()
    whole = grecv[0]
    for s in range(1, spaces):
        whole = whole + grecv[s]

    gram_ref[...] = whole
    for copy in gcopies:
        copy.wait_send()


def finish(blocks, gram_ref, split_ref, modes_ref, factor_ref, held, sem):
    two = 2 * blocks
    loads = []
    for comp in range(COMPS):
        load = pltpu.make_async_copy(split_ref.at[comp], held.at[comp], sem.at[comp])
        load.start()
        loads.append(load)
    whole = gram_ref[...]
    row = lax.broadcasted_iota(jnp.int32, (blocks, two), 0)
    lane = lax.broadcasted_iota(jnp.int32, (blocks, two), 1)
    unit = (lane == row + blocks).astype(F32)
    left = lane < blocks
    re = jnp.where(left, whole[:, :two], unit)
    im = jnp.where(left, jnp.concatenate([whole[:, blocks:two], whole[:, :blocks]], axis=1), 0.0)
    for j in range(blocks - 1):
        inverse = 1.0 / re[j:j + 1, j:j + 1]
        row_re, row_im = re[j:j + 1] * inverse, im[j:j + 1] * inverse
        below = row > j
        col_re = jnp.where(below, re[:, j:j + 1], 0.0)
        col_im = jnp.where(below, im[:, j:j + 1], 0.0)
        re, im = re - (col_re * row_re - col_im * row_im), im - (col_re * row_im + col_im * row_re)
    pivots = jnp.sum(jnp.where(lane == row, re, 0.0), axis=1, keepdims=True)
    scale = 1.0 / jnp.sqrt(pivots)
    re, im = re * scale, im * scale
    factor_ref[0] = jnp.where(lane >= row, re, 0.0)[:, :blocks]
    factor_ref[1] = jnp.where(lane > row, im, 0.0)[:, :blocks]
    wr, wi = re[:, blocks:], im[:, blocks:]
    upper = jnp.concatenate([wr, wi], axis=1)
    lower = jnp.concatenate([-wi, wr], axis=1)
    mixed = jnp.concatenate([src[b:b + 1] for b in range(blocks) for src in (upper, lower)], axis=0)
    m1, m2, m3 = split3(mixed)
    weights = jnp.concatenate([m1, m1, m2, m2, m1, m3], axis=1)
    for comp in range(COMPS):
        loads[comp].wait()
        x1, x2, x3 = (held[comp, i * two:(i + 1) * two] for i in range(3))
        out = jnp.dot(weights, jnp.concatenate([x1, x2, x1, x2, x3, x1], axis=0), preferred_element_type=F32)
        for b in range(blocks):
            modes_ref[b, comp] = out[2 * b:2 * b + 2].astype(BF16)


def solution(mesh):
    count, spaces = mesh.shape["freq"], mesh.shape["space"]
    pairs = count // 2

    def per_device(record, area_weight, freq_bins):
        points = record.shape[2]
        cols = points // CUTS
        chunks = COMPS * CUTS
        two = 2 * count
        lanes = max(128, two)
        dma = pltpu.SemaphoreType.DMA
        split, gram = pl.pallas_call(
            functools.partial(kernel, pairs, spaces),
            out_shape=(
                jax.ShapeDtypeStruct((COMPS, 3 * two, points), BF16),
                jax.ShapeDtypeStruct((count, lanes), F32),
            ),
            in_specs=[
                pl.BlockSpec(memory_space=pltpu.SMEM),
                pl.BlockSpec(memory_space=pl.ANY),
                pl.BlockSpec(memory_space=pl.ANY),
            ],
            out_specs=(pl.BlockSpec(memory_space=pl.ANY), pl.BlockSpec(memory_space=pltpu.VMEM)),
            scratch_shapes=[
                pltpu.VMEM((chunks, HALF, cols), F32),
                pltpu.VMEM((1, points), F32),
                pltpu.VMEM((chunks, 4 * pairs, cols), F32),
                pltpu.VMEM((chunks, 4 * pairs, cols), F32),
                pltpu.VMEM((chunks, 2 * pairs, cols), F32),
                pltpu.VMEM((chunks, pairs, 3, 2, cols), F32),
                pltpu.VMEM((chunks, pairs, 3, 2, cols), F32),
                pltpu.VMEM((chunks, 3 * two, cols), BF16),
                pltpu.VMEM((count, lanes), F32),
                pltpu.VMEM((spaces, count, lanes), F32),
                dma((chunks,)), dma, dma((chunks,)),
                dma((chunks,)), dma((chunks,)),
                dma((chunks, pairs)), dma((chunks, pairs)),
                dma((chunks, pairs)), dma((chunks, pairs)),
                dma((spaces,)), dma((spaces,)),
            ],
            compiler_params=pltpu.CompilerParams(
                collective_id=0, has_side_effects=True, vmem_limit_bytes=56 * 1024 * 1024),
        )(freq_bins, area_weight.reshape(1, points), record.transpose(1, 0, 2))
        modes, factor = pl.pallas_call(
            functools.partial(finish, count),
            out_shape=(
                jax.ShapeDtypeStruct((count, COMPS, 2, points), BF16),
                jax.ShapeDtypeStruct((2, count, count), F32),
            ),
            in_specs=[pl.BlockSpec(memory_space=pltpu.VMEM), pl.BlockSpec(memory_space=pl.ANY)],
            out_specs=(pl.BlockSpec(memory_space=pltpu.VMEM), pl.BlockSpec(memory_space=pltpu.VMEM)),
            scratch_shapes=[pltpu.VMEM((COMPS, 3 * two, points), BF16), dma((COMPS,))],
            compiler_params=pltpu.CompilerParams(vmem_limit_bytes=56 * 1024 * 1024),
        )(gram, split)
        return modes.transpose(0, 2, 1, 3)[None], factor[None]

    return jax.shard_map(
        per_device,
        mesh=mesh,
        in_specs=(P("freq", None, "space"), P("space"), P()),
        out_specs=(P("freq", None, None, None, "space"), P("freq", None, None, None)),
        check_vma=False,
    )
```
